256 devices in a mesh: replica: 4 (over y_lo, core), fsdp: 64 (over z, x, y_hi).
Axes of the slice: x: 4, y: 4 (y_hi: 2, y_lo: 2; y = y_hi * 2 + y_lo), z: 8, core: 2. Of those that a mesh axis runs over, the one named last changes fastest.
Arguments:
- features: bfloat16 [4, 2, 16384, 2304], P('replica', None, 'fsdp'), may hold values from -6 to 6
- queries: bfloat16 [4, 2, 16384, 2048], P('replica', None, 'fsdp'), may hold values from -6 to 6
- values: bfloat16 [4, 2, 16384, 1024], P('replica', None, 'fsdp'), may hold values from -6 to 6
- out_grad: bfloat16 [4, 2, 16384, 2048], P('replica', None, 'fsdp'), may hold values from -6 to 6
- doc_ids: int32 [4, 2, 16384], P('replica', None, 'fsdp'), may hold values from 0 to 255, never falling along the last dimension, each value on 1 to 256 neighbouring positions
- fragment: int32 [1], replicated, may hold values from 0 to 16383
- local_weight: float32 [4, 2304, 1024], P('replica', 'fsdp'), may hold values from -6 to 6
- first_moment: float32 [4, 2304, 1024], P('replica', 'fsdp'), may hold values from -1.5 to 1.5
- second_moment: float32 [4, 2304, 1024], P('replica', 'fsdp'), may hold values from 0.01 to 1
- global_weight: float32 [2304, 1024], P('fsdp'), may hold values from -6 to 6
- outer_momentum: float32 [2304, 1024], P('fsdp'), may hold values from -4 to 4
- outer_delta: float32 [4, 2304, 1024], P('replica', 'fsdp'), may hold values from -4 to 4
Outputs:
- new_local: float32 [4, 2304, 1024], P('replica', 'fsdp')
- new_first: float32 [4, 2304, 1024], P('replica', 'fsdp')
- new_second: float32 [4, 2304, 1024], P('replica', 'fsdp')
- new_global: float32 [2304, 1024], P('fsdp')
- new_momentum: float32 [2304, 1024], P('fsdp')
The draws below stay inside these ranges and needn't reach their ends.
Inputs may be any that keep to these rules, and one draw needn't show every extreme that they name: `doc_ids`: document numbers never fall along the tokens of a replica and step; a document holds 1 to 256 tokens.
All inputs are finite; a program needn't handle non-finite values.
Results may differ from the reference program's by a relative error of at most 0.008.
Values may be sent and summed in bfloat16 or wider, within the bound.
No kernel may reach another device: no remote copies, remote signals or barrier semaphores. Data moves between devices by JAX's collectives and lax.ppermute only.
A program may use at most 128 MiB of HBM per device.

```python
import math
import jax
import jax.numpy as jnp
import numpy as np
from jax import lax

D = 2304
Q_HEADS = 16
KV_HEADS = 8
HEAD = 128
SEQ = 256
STEPS = 2
FRAGS = 4
REPLICAS = 4
TOKENS = 16384
N_REPLICA = 4


def levels(rng, shape, split, least, top_value):
    gain = 1.0
    for dim, parts in split:
        heights = jax.random.uniform(jax.random.fold_in(jax.random.fold_in(rng, 6), dim), (parts,), jnp.float32, least / len(split), top_value / len(split))
        gain = gain * jnp.repeat(jnp.exp(heights), shape[dim] // parts).reshape((-1,) + (1,) * (len(shape) - 1 - dim))
    return gain


def split_up(amount, total, most, slope):
    weights = [(1 << 20) // math.isqrt(grade ** slope) + 1 for grade in range(2, amount + 1)]
    spare, counts = total - most - (amount - 1), [1] * (amount - 1)
    while spare > 0:
        candidates = [i for i in range(amount - 1) if counts[i] < most]
        pool, budget = sum([weights[i] for i in candidates]), spare
        for i in candidates:
            addition = min(most - counts[i], max(1, budget * weights[i] // pool), spare)
            counts[i] = counts[i] + addition
            spare = spare - addition
    return np.array([most] + counts)


def ragged_sizes(own_key, number_of, total, reach, skew):
    if number_of == 2:
        one = jax.random.randint(own_key, (), max(1, total - reach), min(reach, total - 1) + 1)
        return jnp.stack([one, total - one])
    sizes = jnp.asarray(split_up(number_of, total, reach, skew), jnp.int32)
    pairs = (number_of - 1) // 2
    donor, receiver = sizes[1:1 + 2 * pairs:2], sizes[2:2 + 2 * pairs:2]
    room = jnp.minimum(donor - 1, reach - receiver)
    passed = jax.random.randint(jax.random.fold_in(own_key, 1), (pairs,), 0, 1 << 20) % (room + 1)
    sizes = sizes.at[1:1 + 2 * pairs:2].set(donor - passed).at[2:2 + 2 * pairs:2].set(receiver + passed)
    return sizes[jax.random.permutation(jax.random.fold_in(own_key, 2), number_of)]


def bell_draw(own_key, extent, width, most, shards=(), dtype=jnp.bfloat16):
    level = levels(own_key, extent, shards, -0.22, 0.18) if shards else 1.0
    array = jax.random.normal(own_key, extent, jnp.float32) * width * level
    return jnp.minimum(jnp.maximum(array, -most), most).astype(dtype)


def setup_inputs(seed: int = 0) -> dict:
    seeds = jax.random.split(jax.random.key(seed), 13)
    features = bell_draw(seeds[0], (REPLICAS, STEPS, TOKENS, D), 1.0, 6.0, ((0, 4), (2, 64)))
    queries = bell_draw(seeds[1], (REPLICAS, STEPS, TOKENS, Q_HEADS * HEAD), 1.0, 6.0, ((0, 4), (2, 64)))
    values = bell_draw(seeds[2], (REPLICAS, STEPS, TOKENS, KV_HEADS * HEAD), 1.0, 6.0, ((0, 4), (2, 64)))
    out_grad = bell_draw(seeds[3], (REPLICAS, STEPS, TOKENS, Q_HEADS * HEAD), 1.0, 6.0, ((0, 4), (2, 64)))
    doc_ids = jax.vmap(lambda own: jnp.searchsorted(jnp.cumsum(ragged_sizes(own, 4 * TOKENS // SEQ, TOKENS, SEQ, 0)), jnp.arange(TOKENS), side="right"))(jax.random.split(seeds[4], REPLICAS * STEPS)).reshape((REPLICAS, STEPS, TOKENS)).astype(jnp.int32)
    fragment = jax.random.randint(seeds[5], (1,), 0, 4096 * FRAGS).astype(jnp.int32)
    local_weight = bell_draw(seeds[6], (REPLICAS, D, KV_HEADS * HEAD), 1.0, 6.0, ((0, 4), (1, 64)), jnp.float32)
    first_moment = bell_draw(seeds[7], (REPLICAS, D, KV_HEADS * HEAD), 0.1, 1.5, ((0, 4), (1, 64)), jnp.float32)
    second_moment = jnp.clip(jnp.exp(math.log(1.0) - 4.6051702 * jax.random.uniform(seeds[8], (REPLICAS, D, KV_HEADS * HEAD), jnp.float32) ** levels(seeds[8], (REPLICAS, D, KV_HEADS * HEAD), ((0, 4), (1, 64)), -0.2, 0.2)), 0.01, 1.0)
    global_weight = bell_draw(seeds[9], (D, KV_HEADS * HEAD), 1.0, 6.0, ((0, 64),), jnp.float32)
    outer_momentum = bell_draw(seeds[10], (D, KV_HEADS * HEAD), 0.3, 4.0, ((0, 64),), jnp.float32)
    outer_delta = bell_draw(seeds[11], (REPLICAS, D, KV_HEADS * HEAD), 0.3, 4.0, ((0, 4), (1, 64)), jnp.float32)
    return {"features": features, "queries": queries, "values": values, "out_grad": out_grad, "doc_ids": doc_ids, "fragment": fragment, "local_weight": local_weight, "first_moment": first_moment, "second_moment": second_moment, "global_weight": global_weight, "outer_momentum": outer_momentum, "outer_delta": outer_delta}


LEARN_RATE = 0.1
DECAY_RATE = 0.1
BETA_ONE = 0.9
BETA_TWO = 0.999
EPSILON = 1e-08
OUTER_MU = 0.9
OUTER_RATE = 0.7
MERGE_RATE = 0.5
SOFT_CAP = 50.0
QUERY_SCALE = 1.0 / 12.0

def key_cotangent(queries, keys, values, out_grad, docs):
    length = queries.shape[0]
    kv_heads = keys.shape[1] // HEAD
    group = queries.shape[1] // keys.shape[1]
    query_heads = queries.reshape(length, kv_heads, group, HEAD).astype(jnp.float32)
    key_heads = keys.reshape(length, kv_heads, HEAD).astype(jnp.float32)
    value_heads = values.reshape(length, kv_heads, HEAD).astype(jnp.float32)
    grad_heads = out_grad.reshape(length, kv_heads, group, HEAD).astype(jnp.float32)
    raw = jnp.einsum('ikgd,jkd->kgij', query_heads, key_heads) * QUERY_SCALE
    capped = jnp.tanh(raw / SOFT_CAP)
    places = jnp.arange(length)
    allowed = (places[None, :] <= places[:, None]) & (docs[:, None] == docs[None, :])
    expo = jnp.where(allowed, jnp.exp(SOFT_CAP * capped), jnp.float32(0.0))
    probs = expo / lax.optimization_barrier(jnp.sum(expo, axis=-1, keepdims=True))
    dprob = jnp.einsum('ikgd,jkd->kgij', grad_heads, value_heads)
    inner = lax.optimization_barrier(jnp.sum(probs * dprob, axis=-1, keepdims=True))
    dscore = (probs * (dprob - inner) * (1.0 - capped * capped)).astype(jnp.bfloat16)
    dkeys = jnp.einsum('kgij,ikgd->jkd', dscore.astype(jnp.float32), query_heads) * QUERY_SCALE
    return dkeys.reshape(length, kv_heads * HEAD).astype(jnp.bfloat16)

def reference(features, queries, values, out_grad, doc_ids, fragment, local_weight, first_moment, second_moment, global_weight, outer_momentum, outer_delta):
    factor = D ** (-0.5)
    columns = KV_HEADS * HEAD
    frag_cols = columns // FRAGS
    start = (fragment[0] % FRAGS * frag_cols).astype(jnp.int32)
    mean = lax.optimization_barrier(jnp.sum(lax.dynamic_slice_in_dim(outer_delta, start, frag_cols, 2), axis=0)) / N_REPLICA
    old_moment = lax.dynamic_slice_in_dim(outer_momentum, start, frag_cols, 1)
    old_global = lax.dynamic_slice_in_dim(global_weight, start, frag_cols, 1)
    fresh_moment = OUTER_MU * old_moment + mean
    fresh_global = old_global - OUTER_RATE * (mean + OUTER_MU * fresh_moment)
    new_global = lax.dynamic_update_slice_in_dim(global_weight, fresh_global, start, 1)
    new_momentum = lax.dynamic_update_slice_in_dim(outer_momentum, fresh_moment, start, 1)
    locals_out, firsts, seconds = ([], [], [])
    for replica in range(N_REPLICA):
        weight = local_weight[replica]
        moment = first_moment[replica]
        second = second_moment[replica]
        for step in range(STEPS):
            inputs = features[replica, step]
            keys = (jnp.dot(inputs, weight.astype(jnp.bfloat16), preferred_element_type=jnp.float32) * factor).astype(jnp.bfloat16)
            pieces = (queries[replica, step].reshape(-1, SEQ, Q_HEADS * HEAD), keys.reshape(-1, SEQ, columns), values[replica, step].reshape(-1, SEQ, columns), out_grad[replica, step].reshape(-1, SEQ, Q_HEADS * HEAD), doc_ids[replica, step].reshape(-1, SEQ))
            dkeys = lax.map(lambda part: key_cotangent(*part), pieces).reshape(TOKENS, columns)
            grad = jnp.dot(inputs.T, dkeys, preferred_element_type=jnp.float32) * factor
            moment = BETA_ONE * moment + (1.0 - BETA_ONE) * grad
            second = BETA_TWO * second + (1.0 - BETA_TWO) * grad * grad
            weight = weight - LEARN_RATE * (moment / (jnp.sqrt(second) + EPSILON) + DECAY_RATE * weight)
        local_frag = lax.dynamic_slice_in_dim(weight, start, frag_cols, 1)
        merged = MERGE_RATE * local_frag + (1.0 - MERGE_RATE) * fresh_global
        weight = lax.dynamic_update_slice_in_dim(weight, merged, start, 1)
        locals_out.append(weight)
        firsts.append(moment)
        seconds.append(second)
    return (jnp.stack(locals_out), jnp.stack(firsts), jnp.stack(seconds), new_global, new_momentum)
```

```python
import functools

import jax
import jax.numpy as jnp
from jax import lax
from jax.experimental import pallas as pl
from jax.experimental.pallas import tpu as pltpu
from jax.sharding import Mesh
from jax.sharding import PartitionSpec as P

HEAD = 128
STEPS = 2
FRAGS = 4
GROUP = 2
WIDE = 256

LEARN_RATE = 0.1
DECAY_RATE = 0.1
BETA_ONE = 0.9
BETA_TWO = 0.999
EPSILON = 1e-08
OUTER_MU = 0.9
OUTER_RATE = 0.7
MERGE_RATE = 0.5
SOFT_CAP = 50.0
QUERY_SCALE = 1.0 / 12.0

FSDP = ("z", "x", "yh")
REPLICA = ("yl", "core")


def shift(array, axis, by):
    size = lax.axis_size(axis)
    return lax.ppermute(array, axis, [(i, (i + by) % size) for i in range(size)])


def dot(a, b, dims):
    return lax.dot_general(a, b, (dims, ((), ())), preferred_element_type=jnp.float32)


def attend(key, query_heads, value, grad_heads, allowed):
    total = None
    for query, grad in zip(query_heads, grad_heads):
        capped = jnp.tanh(dot(key, query, ((1,), (1,))) * (QUERY_SCALE / SOFT_CAP))
        expo = jnp.where(allowed, jnp.exp(SOFT_CAP * capped), 0.0)
        probs = expo * (1.0 / jnp.sum(expo, axis=0, keepdims=True))
        dprob = dot(value, grad, ((1,), (1,)))
        inner = jnp.sum(probs * dprob, axis=0, keepdims=True)
        dscore = (probs * (dprob - inner) * (1.0 - capped * capped)).astype(jnp.bfloat16)
        term = dot(dscore, query, ((1,), (0,)))
        total = term if total is None else total + term
    return (total * QUERY_SCALE).astype(jnp.bfloat16)


def grad_kernel(
    factor, half, f0, f1, ft0, ft1, w, q0, q1, v0, v1, g0, g1, row0, row1, col0, col1, out
):
    weight = w[...]
    dkeys = []
    parts = ((f0, q0, v0, g0, row0, col0), (f1, q1, v1, g1, row1, col1))
    for f, q, v, g, row, col in parts:
        keys = (dot(f[...], weight, ((1,), (0,))) * factor).astype(jnp.bfloat16)
        length = keys.shape[0]
        key_place = lax.broadcasted_iota(jnp.int32, (length, length), 0)
        query_place = lax.broadcasted_iota(jnp.int32, (length, length), 1)
        allowed = (key_place <= query_place) & (row[...] == col[...])
        heads = []
        for h in range(WIDE // HEAD):
            at = lambda ref, i: ref[:, i * HEAD : (i + 1) * HEAD]
            members = range(h * GROUP, (h + 1) * GROUP)
            heads.append(
                attend(
                    keys[:, h * HEAD : (h + 1) * HEAD],
                    [at(q, i) for i in members],
                    at(v, h),
                    [at(g, i) for i in members],
                    allowed,
                )
            )
        dkeys.append(jnp.concatenate(heads, axis=1))
    total = dot(ft0[...], dkeys[0], ((1,), (0,))) + dot(ft1[...], dkeys[1], ((1,), (0,)))
    out[...] = (total * factor).astype(out.dtype)


def weight_term(features, turned, weight, queries, values, grads, docs, half):
    rows, columns = weight.shape
    tokens = features[0].shape[0]
    steps = columns // WIDE
    wide_q = WIDE * GROUP
    whole = lambda shape: pl.BlockSpec(shape, lambda c, half: (0,) * len(shape))
    own = lambda width: pl.BlockSpec((tokens, width), lambda c, half: (0, half[0] * steps + c))
    packed = lambda width, first: pl.BlockSpec(
        (tokens, width), lambda c, half: (0, first // width + c)
    )
    q_end = columns * GROUP
    g_end = 2 * q_end
    kernel = functools.partial(grad_kernel, rows ** (-0.5))
    doc_rows = [doc.reshape(1, tokens) for doc in docs]
    doc_columns = [doc.reshape(tokens, 1) for doc in docs]
    return pl.pallas_call(
        kernel,
        grid_spec=pltpu.PrefetchScalarGridSpec(
            num_scalar_prefetch=1,
            grid=(steps,),
            in_specs=[
                whole((tokens, rows)),
                whole((tokens, rows)),
                whole((rows, tokens)),
                whole((rows, tokens)),
                pl.BlockSpec((rows, WIDE), lambda c, half: (0, c)),
                own(wide_q),
                packed(wide_q, 0),
                own(WIDE),
                packed(WIDE, g_end),
                own(wide_q),
                packed(wide_q, q_end),
                whole((1, tokens)),
                whole((1, tokens)),
                whole((tokens, 1)),
                whole((tokens, 1)),
            ],
            out_specs=pl.BlockSpec((rows, WIDE), lambda c, half: (0, c)),
        ),
        out_shape=jax.ShapeDtypeStruct((rows, columns), jnp.bfloat16),
        compiler_params=pltpu.CompilerParams(vmem_limit_bytes=48 * 1024 * 1024),
        cost_estimate=pl.CostEstimate(
            flops=8 * tokens * rows * columns + 24 * tokens * tokens * columns,
            bytes_accessed=20 * 1024 * 1024,
            transcendentals=8 * tokens * tokens * columns // HEAD,
        ),
    )(
        half,
        *features,
        *turned,
        weight,
        queries[0],
        queries[1],
        values[0],
        values[1],
        grads[0],
        grads[1],
        *doc_rows,
        *doc_columns,
    )


def gather_rows(block):
    x = lax.axis_index("x")
    size = lax.axis_size("x")
    found = [block] + [shift(block, "x", by) for by in range(1, size)]
    turned = jnp.stack([found[(size - i) % size] for i in range(size)] * 2)
    ordered = lax.dynamic_slice_in_dim(turned, (size - x) % size, size, 0)
    ordered = ordered.reshape(size * block.shape[0], block.shape[1])
    return lax.all_gather(ordered, "z", axis=0, tiled=True)


def scatter_rows(term):
    x = lax.axis_index("x")
    size = lax.axis_size("x")
    part = lax.psum_scatter(term, "z", scatter_dimension=0, tiled=True)
    part = part.reshape(size, part.shape[0] // size, part.shape[1])
    total = lax.dynamic_index_in_dim(part, x, 0, False).astype(jnp.float32)
    for by in range(1, size):
        sent = lax.dynamic_index_in_dim(part, (x + by) % size, 0, False)
        total = total + shift(sent, "x", by).astype(jnp.float32)
    return total


def adam(weight, moment, second, grad):
    moment = BETA_ONE * moment + (1.0 - BETA_ONE) * grad
    second = BETA_TWO * second + (1.0 - BETA_TWO) * grad * grad
    weight = weight - LEARN_RATE * (moment / (jnp.sqrt(second) + EPSILON) + DECAY_RATE * weight)
    return weight, moment, second


def outer_merge(fragment, global_weight, outer_momentum, outer_delta):
    frag_cols = global_weight.shape[1] // FRAGS
    start = fragment[0] % FRAGS * frag_cols
    piece = lax.dynamic_slice_in_dim(outer_delta[0], start, frag_cols, 1)
    old_global = lax.dynamic_slice_in_dim(global_weight, start, frag_cols, 1)
    old_moment = lax.dynamic_slice_in_dim(outer_momentum, start, frag_cols, 1)
    count = 1
    for axis in REPLICA:
        piece = piece + shift(piece, axis, 1)
        count *= lax.axis_size(axis)
    mean = piece / count
    fresh_moment = OUTER_MU * old_moment + mean
    fresh_global = old_global - OUTER_RATE * (mean + OUTER_MU * fresh_moment)
    new_global = lax.dynamic_update_slice_in_dim(global_weight, fresh_global, start, 1)
    new_momentum = lax.dynamic_update_slice_in_dim(outer_momentum, fresh_moment, start, 1)
    return (start, fresh_global, new_global, new_momentum)


def on_device(
    features,
    queries,
    values,
    out_grad,
    doc_ids,
    fragment,
    local_weight,
    first_moment,
    second_moment,
    global_weight,
    outer_momentum,
    outer_delta,
):
    yh = lax.axis_index("yh")
    half = yh.astype(jnp.int32).reshape(1)
    columns = local_weight.shape[2] // 2
    owned = local_weight.shape[1]

    def mine(array, wide=columns):
        return lax.dynamic_slice_in_dim(array, yh * wide, wide, array.ndim - 1)

    def theirs(array, wide=columns):
        return lax.dynamic_slice_in_dim(array, (1 - yh) * wide, wide, array.ndim - 1)

    def paired(array):
        got = shift(theirs(array), "yh", 1)
        kept = mine(array)
        first = jnp.where(yh == 0, kept, got)
        last = jnp.where(yh == 0, got, kept)
        return jnp.concatenate([first, last], axis=0)

    weight, moment, second = local_weight[0], first_moment[0], second_moment[0]
    rows = gather_rows(paired(weight.astype(jnp.bfloat16)))

    docs = shift(doc_ids[0], "yh", 1)
    others = []
    for step in range(STEPS):
        pack = jnp.concatenate(
            [
                theirs(queries[0, step], columns * GROUP),
                theirs(out_grad[0, step], columns * GROUP),
                theirs(values[0, step]),
            ],
            axis=1,
        )
        others.append((shift(features[0, step], "yh", 1), shift(pack, "yh", 1)))

    state = None
    for step in range(STEPS):
        other_features, pack = others[step]
        both = (features[0, step], other_features)
        term = weight_term(
            both,
            [f.T for f in both],
            rows,
            (queries[0, step], pack),
            (values[0, step], pack),
            (out_grad[0, step], pack),
            (doc_ids[0, step], docs[step]),
            half,
        )
        grad = scatter_rows(term)
        if step + 1 < STEPS:
            if state is None:
                state = tuple(paired(a) for a in (weight, moment, second))
            state = adam(*state, grad)
            rows = gather_rows(state[0].astype(jnp.bfloat16))
        kept = jnp.where(yh == 0, grad[:owned], grad[owned:])
        sent = jnp.where(yh == 0, grad[owned:], grad[:owned])
        got = shift(sent, "yh", 1)
        left = jnp.where(yh == 0, kept, got)
        right = jnp.where(yh == 0, got, kept)
        own_grad = jnp.concatenate([left, right], axis=1)
        weight, moment, second = adam(weight, moment, second, own_grad)

    outcome = outer_merge(fragment, global_weight, outer_momentum, outer_delta)
    start, fresh_global, new_global, new_momentum = outcome
    frag_cols = fresh_global.shape[1]
    local_frag = lax.dynamic_slice_in_dim(weight, start, frag_cols, 1)
    merged = MERGE_RATE * local_frag + (1.0 - MERGE_RATE) * fresh_global
    weight = lax.dynamic_update_slice_in_dim(weight, merged, start, 1)
    return (weight[None], moment[None], second[None], new_global, new_momentum)


def solution(mesh):
    lattice = Mesh(mesh.devices.reshape(2, 2, 8, 4, 2), REPLICA + FSDP)
    tokens = P(REPLICA, None, FSDP, None)
    shards = P(REPLICA, FSDP, None)
    return jax.shard_map(
        on_device,
        mesh=lattice,
        in_specs=(
            tokens,
            tokens,
            tokens,
            tokens,
            P(REPLICA, None, FSDP),
            P(),
            shards,
            shards,
            shards,
            P(FSDP, None),
            P(FSDP, None),
            shards,
        ),
        out_specs=(shards, shards, shards, P(FSDP, None), P(FSDP, None)),
        check_vma=False,
    )
```

```python
import functools
import itertools

import jax
import jax.numpy as jnp
from jax import lax
from jax.experimental import pallas as pl
from jax.experimental.pallas import tpu as pltpu
from jax.sharding import Mesh
from jax.sharding import PartitionSpec as P

HEAD = 128
STEPS = 2
FRAGS = 4
GROUP = 2
WIDE = 256

LEARN_RATE = 0.1
DECAY_RATE = 0.1
BETA_ONE = 0.9
BETA_TWO = 0.999
EPSILON = 1e-08
OUTER_MU = 0.9
OUTER_RATE = 0.7
MERGE_RATE = 0.5
SOFT_CAP = 50.0
QUERY_SCALE = 1.0 / 12.0

FSDP = ("z", "x", "yh")
REPLICA = ("yl", "core")


def shift(array, axis, by):
    size = lax.axis_size(axis)
    return lax.ppermute(array, axis, [(i, (i + by) % size) for i in range(size)])


def dot(a, b, dims):
    return lax.dot_general(a, b, (dims, ((), ())), preferred_element_type=jnp.float32)


def attend(key, query_heads, value, grad_heads, allowed):
    total = None
    for query, grad in zip(query_heads, grad_heads):
        capped = jnp.tanh(dot(key, query, ((1,), (1,))) * (QUERY_SCALE / SOFT_CAP))
        expo = jnp.where(allowed, jnp.exp(SOFT_CAP * capped), 0.0)
        probs = expo * (1.0 / jnp.sum(expo, axis=0, keepdims=True))
        dprob = dot(value, grad, ((1,), (1,)))
        inner = jnp.sum(probs * dprob, axis=0, keepdims=True)
        dscore = (probs * (dprob - inner) * (1.0 - capped * capped)).astype(jnp.bfloat16)
        term = dot(dscore, query, ((1,), (0,)))
        total = term if total is None else total + term
    return (total * QUERY_SCALE).astype(jnp.bfloat16)


def grad_kernel(factor, count, half, weight, *refs):
    weight = weight[...]
    total = None
    for n in range(count):
        f, ft, q, g, v, row, col = refs[7 * n : 7 * n + 7]
        keys = (dot(f[...], weight, ((1,), (0,))) * factor).astype(jnp.bfloat16)
        length = keys.shape[0]
        key_place = lax.broadcasted_iota(jnp.int32, (length, length), 0)
        query_place = lax.broadcasted_iota(jnp.int32, (length, length), 1)
        allowed = (key_place <= query_place) & (row[...] == col[...])
        at = lambda ref, i: ref[:, i * HEAD : (i + 1) * HEAD]
        heads = []
        for h in range(WIDE // HEAD):
            members = range(h * GROUP, (h + 1) * GROUP)
            heads.append(
                attend(
                    keys[:, h * HEAD : (h + 1) * HEAD],
                    [at(q, i) for i in members],
                    at(v, h),
                    [at(g, i) for i in members],
                    allowed,
                )
            )
        term = dot(ft[...], jnp.concatenate(heads, axis=1), ((1,), (0,)))
        total = term if total is None else total + term
    out = refs[-1]
    out[...] = (total * factor).astype(out.dtype)


def weight_term(weight, sequences, half):
    rows, columns = weight.shape
    tokens = sequences[0][0].shape[0]
    whole = lambda shape: pl.BlockSpec(shape, lambda c, half: (0,) * len(shape))
    block = lambda width, place: pl.BlockSpec((tokens, width), lambda c, half: (0, place(c, half)))
    specs, arrays = [], []
    for f, ft, q, g, v, doc in sequences:
        specs += [
            whole((tokens, rows)),
            whole((rows, tokens)),
            block(WIDE * GROUP, q[1]),
            block(WIDE * GROUP, g[1]),
            block(WIDE, v[1]),
            whole((1, tokens)),
            whole((tokens, 1)),
        ]
        arrays += [f, ft, q[0], g[0], v[0], doc.reshape(1, tokens), doc.reshape(tokens, 1)]
    tile = pl.BlockSpec((rows, WIDE), lambda c, half: (0, c))
    count = len(sequences)
    return pl.pallas_call(
        functools.partial(grad_kernel, rows ** (-0.5), count),
        grid_spec=pltpu.PrefetchScalarGridSpec(
            num_scalar_prefetch=1,
            grid=(columns // WIDE,),
            in_specs=[tile] + specs,
            out_specs=tile,
        ),
        out_shape=jax.ShapeDtypeStruct((rows, columns), jnp.bfloat16),
        compiler_params=pltpu.CompilerParams(vmem_limit_bytes=56 * 1024 * 1024),
        cost_estimate=pl.CostEstimate(
            flops=4 * count * tokens * rows * columns + 12 * count * tokens * tokens * columns,
            bytes_accessed=4 * count * 1024 * 1024,
            transcendentals=4 * count * tokens * tokens * columns // HEAD,
        ),
    )(half, weight, *arrays)


def from_all(block, axis, stride):
    size = lax.axis_size(axis) // stride
    me = lax.axis_index(axis) // stride
    found = jnp.stack([block] + [shift(block, axis, by * stride) for by in range(1, size)])
    return [lax.dynamic_index_in_dim(found, (me - i) % size, 0, False) for i in range(size)]


def sum_for(pieces, axis, stride):
    size = lax.axis_size(axis) // stride
    me = lax.axis_index(axis) // stride
    sent = [shift(pieces((me + by) % size), axis, by * stride) for by in range(1, size)]
    total = pieces(me).astype(jnp.float32)
    for got in sent:
        total = total + got.astype(jnp.float32)
    return total


def gather_rows(block):
    columns = block.shape[-1]
    found = jnp.stack(from_all(block, "z", 2))
    return jnp.stack(from_all(found, "x", 1), axis=2).reshape(-1, columns)


def scatter_rows(term):
    term = term.reshape(lax.axis_size("z"), lax.axis_size("x"), -1, term.shape[1])
    part = sum_for(lambda i: lax.dynamic_index_in_dim(term, i, 1, False), "x", 1)
    part = part.astype(jnp.bfloat16)
    return sum_for(lambda i: lax.dynamic_slice_in_dim(part, 2 * i, 2, 0), "z", 2)


def route(array, move):
    axes = ("core", "z", "yh")
    sizes = [lax.axis_size(axis) for axis in axes]
    flat = lambda c, z, h: (c * sizes[1] + z) * sizes[2] + h
    places = itertools.product(*[range(size) for size in sizes])
    return lax.ppermute(array, axes, [(flat(*p), flat(*move(*p))) for p in places])


def swap(array):
    return route(array, lambda c, z, h: (h, z, c))


def to_core(array):
    return route(array, lambda c, z, h: (1 - c, z, h))


def to_pair(array):
    return route(array, lambda c, z, h: (c, z ^ 1, h))


MEMBERS = 4


def hand_out(array):
    wide = array.shape[-1] // MEMBERS
    zp = lax.axis_index("z") % 2
    owner = 2 * zp + lax.axis_index("yh")
    found = []
    for t in range(MEMBERS):
        part = lax.dynamic_slice_in_dim(array, (owner ^ t) * wide, wide, array.ndim - 1)
        found.append(route(part, lambda c, z, h: (h ^ (t & 1), z ^ (t >> 1), c)))
    found = jnp.stack(found)
    member = 2 * zp + lax.axis_index("core")
    return jnp.stack(
        [lax.dynamic_index_in_dim(found, member ^ j, 0, False) for j in range(MEMBERS)]
    )


def hand_back(blocks):
    zp = lax.axis_index("z") % 2
    member = 2 * zp + lax.axis_index("core")
    found = []
    for t in range(MEMBERS):
        part = lax.dynamic_index_in_dim(blocks, member ^ t, 0, False)
        found.append(route(part, lambda c, z, h: (h, z ^ (t >> 1), c ^ (t & 1))))
    found = jnp.stack(found)
    owner = 2 * zp + lax.axis_index("yh")
    return jnp.concatenate(
        [lax.dynamic_index_in_dim(found, owner ^ j, 0, False) for j in range(MEMBERS)], axis=1
    )


def adam(weight, moment, second, grad):
    moment = BETA_ONE * moment + (1.0 - BETA_ONE) * grad
    second = BETA_TWO * second + (1.0 - BETA_TWO) * grad * grad
    weight = weight - LEARN_RATE * (moment / (jnp.sqrt(second) + EPSILON) + DECAY_RATE * weight)
    return weight, moment, second


def outer_merge(fragment, global_weight, outer_momentum, outer_delta):
    frag_cols = global_weight.shape[1] // FRAGS
    start = fragment[0] % FRAGS * frag_cols
    piece = lax.dynamic_slice_in_dim(outer_delta[0], start, frag_cols, 1)
    old_global = lax.dynamic_slice_in_dim(global_weight, start, frag_cols, 1)
    old_moment = lax.dynamic_slice_in_dim(outer_momentum, start, frag_cols, 1)
    count = 1
    for axis in REPLICA:
        piece = piece + shift(piece, axis, 1)
        count *= lax.axis_size(axis)
    mean = piece / count
    fresh_moment = OUTER_MU * old_moment + mean
    fresh_global = old_global - OUTER_RATE * (mean + OUTER_MU * fresh_moment)
    new_global = lax.dynamic_update_slice_in_dim(global_weight, fresh_global, start, 1)
    new_momentum = lax.dynamic_update_slice_in_dim(outer_momentum, fresh_moment, start, 1)
    return (start, fresh_global, new_global, new_momentum)


def on_device(
    features,
    queries,
    values,
    out_grad,
    doc_ids,
    fragment,
    local_weight,
    first_moment,
    second_moment,
    global_weight,
    outer_momentum,
    outer_delta,
):
    zp, core = lax.axis_index("z") % 2, lax.axis_index("core")
    member = (2 * zp + core).astype(jnp.int32).reshape(1)
    owned = local_weight.shape[1]
    weight, moment, second = local_weight[0], first_moment[0], second_moment[0]

    def cell_rows(blocks):
        return blocks.reshape(2, 2 * owned, WIDE)

    first_block = cell_rows(hand_out(weight.astype(jnp.bfloat16)))

    def pick(arrays, first, count):
        widths = (GROUP * HEAD, GROUP * HEAD, HEAD)
        parts = [
            lax.dynamic_slice_in_dim(a, first * w, count * w, 1) for a, w in zip(arrays, widths)
        ]
        return jnp.concatenate(parts, axis=1)

    heads = WIDE // HEAD

    def unpack(pack, count):
        q = count * GROUP * HEAD
        return pack[:, :q], pack[:, q : 2 * q], pack[:, 2 * q :]

    def swapped(step):
        return [
            swap(a[0, step]) for a in (features, queries, out_grad, values)
        ], swap(doc_ids[0, step])

    def paired(arrays):
        f, *rest = arrays
        return to_pair(f), to_pair(pick(rest, (1 - zp) * 2 * heads, 2 * heads))

    def shared(arrays, pair, doc):
        f, *rest = arrays
        other_f, pack = pair
        pair_doc = to_pair(doc)
        core_f, both_f = to_core(f), to_core(other_f)
        core_pack = to_core(pick(rest, (zp * 2 + 1 - core) * heads, heads))
        both_pack = to_core(pick(unpack(pack, 2 * heads), (1 - core) * heads, heads))
        here = lambda i, m: m[0]
        turn = lambda a: a.T
        q, g, v = rest
        return [
            (f, turn(f), (q, here), (g, here), (v, here), doc),
            (
                core_f,
                turn(core_f),
                (core_pack, lambda i, m: 0),
                (core_pack, lambda i, m: 1),
                (core_pack, lambda i, m: 2 * GROUP),
                to_core(doc),
            ),
            (
                other_f,
                turn(other_f),
                (pack, lambda i, m: m[0] % 2),
                (pack, lambda i, m: 2 + m[0] % 2),
                (pack, lambda i, m: 4 * GROUP + m[0] % 2),
                pair_doc,
            ),
            (
                both_f,
                turn(both_f),
                (both_pack, lambda i, m: 0),
                (both_pack, lambda i, m: 1),
                (both_pack, lambda i, m: 2 * GROUP),
                to_core(pair_doc),
            ),
        ]

    arrays, doc = swapped(0)
    sequences = shared(arrays, paired(arrays), doc)
    arrays, doc = swapped(1)

    rows = gather_rows(first_block)
    rows, arrays[0], arrays[1] = lax.optimization_barrier((rows, arrays[0], arrays[1]))
    term = weight_term(rows, sequences, member)
    term, arrays[2], arrays[3] = lax.optimization_barrier((term, arrays[2], arrays[3]))
    pair = paired(arrays)
    grad = scatter_rows(term)
    grad, other_f = lax.optimization_barrier((grad, pair[0]))
    pair = (other_f, pair[1])

    state = hand_out(jnp.stack([weight, moment, second]))
    state = [cell_rows(state[:, i]) for i in range(3)]
    fresh = adam(*state, grad)
    rows = gather_rows(fresh[0].astype(jnp.bfloat16))
    own_grad = hand_back(grad.reshape(MEMBERS, owned, WIDE))
    weight, moment, second = adam(weight, moment, second, own_grad)

    term = weight_term(rows, shared(arrays, pair, doc), member)
    own_grad = hand_back(scatter_rows(term).reshape(MEMBERS, owned, WIDE))
    weight, moment, second = adam(weight, moment, second, own_grad)

    outcome = outer_merge(fragment, global_weight, outer_momentum, outer_delta)
    start, fresh_global, new_global, new_momentum = outcome
    frag_cols = fresh_global.shape[1]
    local_frag = lax.dynamic_slice_in_dim(weight, start, frag_cols, 1)
    merged = MERGE_RATE * local_frag + (1.0 - MERGE_RATE) * fresh_global
    weight = lax.dynamic_update_slice_in_dim(weight, merged, start, 1)
    return (weight[None], moment[None], second[None], new_global, new_momentum)


def solution(mesh):
    lattice = Mesh(mesh.devices.reshape(2, 2, 8, 4, 2), REPLICA + FSDP)
    tokens = P(REPLICA, None, FSDP, None)
    shards = P(REPLICA, FSDP, None)
    return jax.shard_map(
        on_device,
        mesh=lattice,
        in_specs=(
            tokens,
            tokens,
            tokens,
            tokens,
            P(REPLICA, None, FSDP),
            P(),
            shards,
            shards,
            shards,
            P(FSDP, None),
            P(FSDP, None),
            shards,
        ),
        out_specs=(shards, shards, shards, P(FSDP, None), P(FSDP, None)),
        check_vma=False,
    )
```

```python
import functools

import jax
import jax.numpy as jnp
from jax import lax
from jax.experimental import pallas as pl
from jax.experimental.pallas import tpu as pltpu
from jax.sharding import Mesh
from jax.sharding import PartitionSpec as P

HEAD = 128
STEPS = 2
FRAGS = 4
GROUP = 2
WIDE = 256

LEARN_RATE = 0.1
DECAY_RATE = 0.1
BETA_ONE = 0.9
BETA_TWO = 0.999
EPSILON = 1e-08
OUTER_MU = 0.9
OUTER_RATE = 0.7
MERGE_RATE = 0.5
SOFT_CAP = 50.0
QUERY_SCALE = 1.0 / 12.0

FSDP = ("z", "x", "yh")
REPLICA = ("yl", "core")


def shift(array, axis, by):
    size = lax.axis_size(axis)
    return lax.ppermute(array, axis, [(i, (i + by) % size) for i in range(size)])


def dot(a, b, dims):
    return lax.dot_general(a, b, (dims, ((), ())), preferred_element_type=jnp.float32)


def attend(key, query_heads, value, grad_heads, allowed):
    total = None
    for query, grad in zip(query_heads, grad_heads):
        capped = jnp.tanh(dot(key, query, ((1,), (1,))) * (QUERY_SCALE / SOFT_CAP))
        expo = jnp.where(allowed, jnp.exp(SOFT_CAP * capped), 0.0)
        probs = expo * (1.0 / jnp.sum(expo, axis=0, keepdims=True))
        dprob = dot(value, grad, ((1,), (1,)))
        inner = jnp.sum(probs * dprob, axis=0, keepdims=True)
        dscore = (probs * (dprob - inner) * (1.0 - capped * capped)).astype(jnp.bfloat16)
        term = dot(dscore, query, ((1,), (0,)))
        total = term if total is None else total + term
    return (total * QUERY_SCALE).astype(jnp.bfloat16)


def grad_kernel(factor, step, place, *refs):
    zs, chunks = 8, 2
    blocks, refs = refs[: zs * chunks], refs[zs * chunks :]
    (f, ft, q, g, v, other_f, other_ft, *packs), refs = refs[: 7 + chunks], refs[7 + chunks :]
    docs, refs = refs[:4], refs[4:]
    outs, refs = refs[: zs * chunks], refs[zs * chunks :]
    weight, f_buf, ft_buf, own_buf, pack_buf, total_ref, sems = refs
    half, z = place[0], place[1]
    share = weight.shape[1] // zs
    wide = WIDE * GROUP
    spot = lambda i: pl.ds(pl.multiple_of(lax.rem(i + zs, zs) * share, share), share)
    copies = []

    def fetch(source, target):
        copies.append(pltpu.make_async_copy(source, target, sems.at[len(copies)]))
        copies[-1].start()
        return copies[-1]

    def fetch_weight(c):
        return [
            fetch(blocks[c * zs + by], weight.at[c, spot(z - by), :]) for by in range(zs)
        ]

    def fetch_own(c):
        start = 0
        found = []
        for source, width in ((q, wide), (g, wide), (v, WIDE)):
            at = pl.multiple_of((half * chunks + c) * width, width)
            found.append(
                fetch(
                    source.at[0, step, :, pl.ds(at, width)],
                    own_buf.at[c, :, start : start + width],
                )
            )
            start += width
        return found

    need = {}
    need["f", 0] = [fetch(f.at[0, step], f_buf.at[0])]
    need["w", 0] = fetch_weight(0)
    need["x", 0, 0] = fetch_own(0)
    need["ft", 0] = [fetch(ft, ft_buf.at[0])]
    need["f", 1] = [fetch(other_f, f_buf.at[1])]
    need["x", 0, 1] = [fetch(packs[0], pack_buf.at[0])]
    need["ft", 1] = [fetch(other_ft, ft_buf.at[1])]
    need["w", 1] = fetch_weight(1)
    need["x", 1, 0] = fetch_own(1)
    need["x", 1, 1] = [fetch(packs[1], pack_buf.at[1])]

    def wait(*key):
        for copy in need.pop(key, ()):
            copy.wait()

    for c in range(chunks):
        for n, buf in enumerate((own_buf, pack_buf)):
            wait("f", n)
            wait("w", c)
            keys = dot(f_buf[n], weight[c], ((1,), (0,)))
            keys = (keys * factor).astype(jnp.bfloat16)
            length = keys.shape[0]
            key_place = lax.broadcasted_iota(jnp.int32, (length, length), 0)
            query_place = lax.broadcasted_iota(jnp.int32, (length, length), 1)
            allowed = (key_place <= query_place) & (docs[n][...] == docs[2 + n][...])
            wait("x", c, n)
            at = lambda start, i: buf[c, :, start + i * HEAD : start + (i + 1) * HEAD]
            heads = []
            for h in range(WIDE // HEAD):
                members = range(h * GROUP, (h + 1) * GROUP)
                heads.append(
                    attend(
                        keys[:, h * HEAD : (h + 1) * HEAD],
                        [at(0, i) for i in members],
                        at(2 * wide, h),
                        [at(wide, i) for i in members],
                        allowed,
                    )
                )
            wait("ft", n)
            term = dot(ft_buf[n], jnp.concatenate(heads, axis=1), ((1,), (0,))) * factor
            total_ref[...] = term if n == 0 else total_ref[...] + term
        for by in range(zs):
            out = outs[c * zs + by]
            out[...] = total_ref[spot(z + by), :].astype(out.dtype)


def weight_terms(step, blocks, own, others, docs, place):
    zs, chunks = len(blocks[0]), len(blocks)
    share, columns = blocks[0][0].shape
    rows = share * zs
    tokens = others[0].shape[0]
    width = columns * (2 * GROUP + 1)
    whole = lambda *shape: pl.BlockSpec(shape, lambda i, p: (0,) * len(shape))
    inputs = [*blocks[0], *blocks[1], *own, *others]
    docs = [d.reshape(1, tokens) for d in docs] + [d.reshape(tokens, 1) for d in docs]
    out = jax.ShapeDtypeStruct((share, columns), jnp.bfloat16)
    found = pl.pallas_call(
        functools.partial(grad_kernel, rows ** (-0.5), step),
        grid_spec=pltpu.PrefetchScalarGridSpec(
            num_scalar_prefetch=1,
            grid=(1,),
            in_specs=[pl.BlockSpec(memory_space=pl.ANY)] * len(inputs)
            + [whole(*d.shape) for d in docs],
            out_specs=[whole(share, columns)] * (zs * chunks),
            scratch_shapes=[
                pltpu.VMEM((chunks, rows, columns), jnp.bfloat16),
                pltpu.VMEM((2, tokens, rows), jnp.bfloat16),
                pltpu.VMEM((2, rows, tokens), jnp.bfloat16),
                pltpu.VMEM((chunks, tokens, width), jnp.bfloat16),
                pltpu.VMEM((chunks, tokens, width), jnp.bfloat16),
                pltpu.VMEM((rows, columns), jnp.float32),
                pltpu.SemaphoreType.DMA((zs * chunks + 3 * chunks + 4 + chunks,)),
            ],
        ),
        out_shape=[out] * (zs * chunks),
        compiler_params=pltpu.CompilerParams(vmem_limit_bytes=58 * 1024 * 1024),
        cost_estimate=pl.CostEstimate(
            flops=16 * tokens * rows * columns + 48 * tokens * tokens * columns,
            bytes_accessed=16 * 1024 * 1024,
            transcendentals=16 * tokens * tokens * columns // HEAD,
        ),
    )(place, *inputs, *docs)
    return [found[:zs], found[zs:]]


def all_x(block):
    x = lax.axis_index("x")
    size = lax.axis_size("x")
    found = jnp.stack([block] + [shift(block, "x", by) for by in range(1, size)])
    return [lax.dynamic_index_in_dim(found, (x - i) % size, 0, False) for i in range(size)]


def sum_for_x(pieces):
    x = lax.axis_index("x")
    size = lax.axis_size("x")
    sent = [shift(pieces((x + by) % size), "x", by) for by in range(1, size)]
    total = pieces(x).astype(jnp.float32)
    for got in sent:
        total = total + got.astype(jnp.float32)
    return total


def ring_gather(block):
    size = lax.axis_size("z")
    found = [block] * size
    up = down = block
    for hop in range(1, size // 2 + 1):
        up = found[hop] = shift(up, "z", 1)
        if 2 * hop < size:
            down = found[size - hop] = shift(down, "z", -1)
    return found


def ring_sum(blocks):
    size = lax.axis_size("z")
    add = lambda a, b: a.astype(jnp.float32) + b.astype(jnp.float32)
    up, down = blocks[size // 2], blocks[size // 2 + 1]
    for hop in range(size // 2, 0, -1):
        up = shift(up, "z", 1)
        if hop > 1:
            up = add(up, blocks[hop - 1]).astype(jnp.bfloat16)
            down = shift(down, "z", -1)
            if hop > 2:
                down = add(down, blocks[size + 2 - hop]).astype(jnp.bfloat16)
    return add(up, down) + blocks[0].astype(jnp.float32)


def adam(weight, moment, second, grad):
    moment = BETA_ONE * moment + (1.0 - BETA_ONE) * grad
    second = BETA_TWO * second + (1.0 - BETA_TWO) * grad * grad
    weight = weight - LEARN_RATE * (moment / (jnp.sqrt(second) + EPSILON) + DECAY_RATE * weight)
    return weight, moment, second


def outer_merge(fragment, global_weight, outer_momentum, outer_delta):
    frag_cols = global_weight.shape[1] // FRAGS
    start = fragment[0] % FRAGS * frag_cols
    piece = lax.dynamic_slice_in_dim(outer_delta[0], start, frag_cols, 1)
    old_global = lax.dynamic_slice_in_dim(global_weight, start, frag_cols, 1)
    old_moment = lax.dynamic_slice_in_dim(outer_momentum, start, frag_cols, 1)
    count = 1
    for axis in REPLICA:
        piece = piece + shift(piece, axis, 1)
        count *= lax.axis_size(axis)
    mean = piece / count
    fresh_moment = OUTER_MU * old_moment + mean
    fresh_global = old_global - OUTER_RATE * (mean + OUTER_MU * fresh_moment)
    new_global = lax.dynamic_update_slice_in_dim(global_weight, fresh_global, start, 1)
    new_momentum = lax.dynamic_update_slice_in_dim(outer_momentum, fresh_moment, start, 1)
    return (start, fresh_global, new_global, new_momentum)


def on_device(
    features,
    queries,
    values,
    out_grad,
    doc_ids,
    fragment,
    local_weight,
    first_moment,
    second_moment,
    global_weight,
    outer_momentum,
    outer_delta,
):
    yh = lax.axis_index("yh")
    place = jnp.stack([yh, lax.axis_index("z")]).astype(jnp.int32)
    columns = local_weight.shape[2] // 2
    owned = local_weight.shape[1]

    def mine(array, wide=columns):
        return lax.dynamic_slice_in_dim(array, yh * wide, wide, array.ndim - 1)

    def theirs(array, wide=columns):
        return lax.dynamic_slice_in_dim(array, (1 - yh) * wide, wide, array.ndim - 1)

    def in_order(kept, got):
        first = jnp.where(yh == 0, kept, got)
        last = jnp.where(yh == 0, got, kept)
        return jnp.concatenate([first, last], axis=0)

    def paired(array):
        return in_order(mine(array), shift(theirs(array), "yh", 1))

    weight, moment, second = local_weight[0], first_moment[0], second_moment[0]

    def after(array, earlier):
        return lax.optimization_barrier((array, earlier))[0]

    def pack(arrays, c):
        widths = (WIDE * GROUP, WIDE * GROUP, WIDE)
        at = (1 - yh) * 2 + c
        parts = [lax.dynamic_slice_in_dim(a, at * w, w, 1) for a, w in zip(arrays, widths)]
        return jnp.concatenate(parts, axis=1)

    def move(step, earlier, later):
        f = shift(after(features[0, step], earlier), "yh", 1)
        arrays = after([a[0, step] for a in (queries, out_grad, values)], later)
        return [f] + [shift(pack(arrays, c), "yh", 1) for c in range(2)]

    def gather(rows):
        return ring_gather(rows[:, :WIDE]), ring_gather(rows[:, WIDE:])

    def terms(step, blocks, others, ready):
        own = (features, after(features[0, step], ready).T, queries, out_grad, values)
        f, *packs = others
        pair_docs = (doc_ids[0, step], docs[step])
        return weight_terms(step, blocks, own, (f, f.T, *packs), pair_docs, place)

    def scatter(blocks, earlier):
        part = jnp.concatenate([ring_sum(b).astype(jnp.bfloat16) for b in blocks], axis=1)
        part = after(part, earlier)
        part = part.reshape(lax.axis_size("x"), -1, part.shape[1])
        return sum_for_x(lambda i: lax.dynamic_index_in_dim(part, i, 0, False))

    def traded(grad):
        kept = jnp.where(yh == 0, grad[:owned], grad[owned:])
        got = shift(jnp.where(yh == 0, grad[owned:], grad[:owned]), "yh", 1)
        left = jnp.where(yh == 0, kept, got)
        right = jnp.where(yh == 0, got, kept)
        return jnp.concatenate([left, right], axis=1)

    sent = theirs(weight.astype(jnp.bfloat16))
    block = in_order(mine(weight.astype(jnp.bfloat16)), shift(sent, "yh", 1))
    docs = shift(after(doc_ids[0], sent), "yh", 1)
    rows = jnp.concatenate(all_x(block))
    first = move(0, sent, rows)
    state = after(jnp.stack([weight, moment, second]), first)
    kept, got = mine(state), shift(theirs(state), "yh", 1)
    state = jnp.concatenate([jnp.where(yh == 0, kept, got), jnp.where(yh == 0, got, kept)], axis=1)
    later = move(1, first, first)
    outer = after((global_weight, outer_momentum, outer_delta), later)
    outcome = outer_merge(fragment, *outer)

    found = terms(0, gather(rows), first, rows)
    grad = scatter(found, later[0])
    fresh = adam(*state, grad)
    rows = jnp.concatenate(all_x(fresh[0].astype(jnp.bfloat16)))
    found = terms(1, gather(after(rows, later[1])), later, found)
    own_grad = traded(after(grad, found))
    weight, moment, second = adam(weight, moment, second, own_grad)
    own_grad = traded(scatter(found, outcome))
    weight, moment, second = adam(weight, moment, second, own_grad)

    start, fresh_global, new_global, new_momentum = outcome
    frag_cols = fresh_global.shape[1]
    local_frag = lax.dynamic_slice_in_dim(weight, start, frag_cols, 1)
    merged = MERGE_RATE * local_frag + (1.0 - MERGE_RATE) * fresh_global
    weight = lax.dynamic_update_slice_in_dim(weight, merged, start, 1)
    return (weight[None], moment[None], second[None], new_global, new_momentum)


def solution(mesh):
    lattice = Mesh(mesh.devices.reshape(2, 2, 8, 4, 2), REPLICA + FSDP)
    tokens = P(REPLICA, None, FSDP, None)
    shards = P(REPLICA, FSDP, None)
    return jax.shard_map(
        on_device,
        mesh=lattice,
        in_specs=(
            tokens,
            tokens,
            tokens,
            tokens,
            P(REPLICA, None, FSDP),
            P(),
            shards,
            shards,
            shards,
            P(FSDP, None),
            P(FSDP, None),
            shards,
        ),
        out_specs=(shards, shards, shards, P(FSDP, None), P(FSDP, None)),
        check_vma=False,
    )
```

```python
import functools

import jax
import jax.numpy as jnp
from jax import lax
from jax.experimental import pallas as pl
from jax.experimental.pallas import tpu as pltpu
from jax.sharding import Mesh
from jax.sharding import PartitionSpec as P

HEAD = 128
STEPS = 2
FRAGS = 4
GROUP = 2
WIDE = 256

LEARN_RATE = 0.1
DECAY_RATE = 0.1
BETA_ONE = 0.9
BETA_TWO = 0.999
EPSILON = 1e-08
OUTER_MU = 0.9
OUTER_RATE = 0.7
MERGE_RATE = 0.5
SOFT_CAP = 50.0
QUERY_SCALE = 1.0 / 12.0

FSDP = ("z", "x", "yh")
REPLICA = ("yl", "core")


def shift(array, axis, by):
    size = lax.axis_size(axis)
    return lax.ppermute(array, axis, [(i, (i + by) % size) for i in range(size)])


def dot(a, b, dims):
    return lax.dot_general(a, b, (dims, ((), ())), preferred_element_type=jnp.float32)


def attend(key, query_heads, value, grad_heads, allowed):
    total = None
    for query, grad in zip(query_heads, grad_heads):
        capped = jnp.tanh(dot(key, query, ((1,), (1,))) * (QUERY_SCALE / SOFT_CAP))
        expo = jnp.where(allowed, jnp.exp(SOFT_CAP * capped), 0.0)
        probs = expo * (1.0 / jnp.sum(expo, axis=0, keepdims=True))
        dprob = dot(value, grad, ((1,), (1,)))
        inner = jnp.sum(probs * dprob, axis=0, keepdims=True)
        dscore = (probs * (dprob - inner) * (1.0 - capped * capped)).astype(jnp.bfloat16)
        term = dot(dscore, query, ((1,), (0,)))
        total = term if total is None else total + term
    return (total * QUERY_SCALE).astype(jnp.bfloat16)


def grad_kernel(factor, step, place, *refs):
    zs, chunks = 8, 2
    blocks, refs = refs[: zs * chunks], refs[zs * chunks :]
    (f, ft, q, g, v, other_f, other_ft, *packs), refs = refs[: 7 + chunks], refs[7 + chunks :]
    docs, refs = refs[:4], refs[4:]
    outs, refs = refs[: zs * chunks], refs[zs * chunks :]
    weight, f_buf, ft_buf, own_buf, pack_buf, total_ref, sems = refs
    half, z = place[0], place[1]
    share = weight.shape[1] // zs
    wide = WIDE * GROUP
    spot = lambda i: pl.ds(pl.multiple_of(lax.rem(i + zs, zs) * share, share), share)
    copies = []

    def fetch(source, target):
        copies.append(pltpu.make_async_copy(source, target, sems.at[len(copies)]))
        copies[-1].start()
        return copies[-1]

    def fetch_weight(c):
        return [
            fetch(blocks[c * zs + by], weight.at[c, spot(z - by), :]) for by in range(zs)
        ]

    def fetch_own(c):
        start = 0
        found = []
        for source, width in ((q, wide), (g, wide), (v, WIDE)):
            at = pl.multiple_of((half * chunks + c) * width, width)
            found.append(
                fetch(
                    source.at[0, step, :, pl.ds(at, width)],
                    own_buf.at[c, :, start : start + width],
                )
            )
            start += width
        return found

    need = {}
    need["f", 0] = [fetch(f.at[0, step], f_buf.at[0])]
    need["w", 0] = fetch_weight(0)
    need["x", 0, 0] = fetch_own(0)
    need["ft", 0] = [fetch(ft, ft_buf.at[0])]
    need["f", 1] = [fetch(other_f, f_buf.at[1])]
    need["x", 0, 1] = [fetch(packs[0], pack_buf.at[0])]
    need["ft", 1] = [fetch(other_ft, ft_buf.at[1])]
    need["w", 1] = fetch_weight(1)
    need["x", 1, 0] = fetch_own(1)
    need["x", 1, 1] = [fetch(packs[1], pack_buf.at[1])]

    def wait(*key):
        for copy in need.pop(key, ()):
            copy.wait()

    for c in range(chunks):
        for n, buf in enumerate((own_buf, pack_buf)):
            wait("f", n)
            wait("w", c)
            keys = dot(f_buf[n], weight[c], ((1,), (0,)))
            keys = (keys * factor).astype(jnp.bfloat16)
            length = keys.shape[0]
            key_place = lax.broadcasted_iota(jnp.int32, (length, length), 0)
            query_place = lax.broadcasted_iota(jnp.int32, (length, length), 1)
            allowed = (key_place <= query_place) & (docs[n][...] == docs[2 + n][...])
            wait("x", c, n)
            at = lambda start, i: buf[c, :, start + i * HEAD : start + (i + 1) * HEAD]
            heads = []
            for h in range(WIDE // HEAD):
                members = range(h * GROUP, (h + 1) * GROUP)
                heads.append(
                    attend(
                        keys[:, h * HEAD : (h + 1) * HEAD],
                        [at(0, i) for i in members],
                        at(2 * wide, h),
                        [at(wide, i) for i in members],
                        allowed,
                    )
                )
            wait("ft", n)
            term = dot(ft_buf[n], jnp.concatenate(heads, axis=1), ((1,), (0,))) * factor
            total_ref[...] = term if n == 0 else total_ref[...] + term
        for by in range(zs):
            out = outs[c * zs + by]
            out[...] = total_ref[spot(z + by), :].astype(out.dtype)


def weight_terms(step, blocks, own, others, docs, place):
    zs, chunks = len(blocks[0]), len(blocks)
    share, columns = blocks[0][0].shape
    rows = share * zs
    tokens = others[0].shape[0]
    width = columns * (2 * GROUP + 1)
    whole = lambda *shape: pl.BlockSpec(shape, lambda i, p: (0,) * len(shape))
    inputs = [*blocks[0], *blocks[1], *own, *others]
    docs = [d.reshape(1, tokens) for d in docs] + [d.reshape(tokens, 1) for d in docs]
    out = jax.ShapeDtypeStruct((share, columns), jnp.bfloat16)
    found = pl.pallas_call(
        functools.partial(grad_kernel, rows ** (-0.5), step),
        grid_spec=pltpu.PrefetchScalarGridSpec(
            num_scalar_prefetch=1,
            grid=(1,),
            in_specs=[pl.BlockSpec(memory_space=pl.ANY)] * len(inputs)
            + [whole(*d.shape) for d in docs],
            out_specs=[whole(share, columns)] * (zs * chunks),
            scratch_shapes=[
                pltpu.VMEM((chunks, rows, columns), jnp.bfloat16),
                pltpu.VMEM((2, tokens, rows), jnp.bfloat16),
                pltpu.VMEM((2, rows, tokens), jnp.bfloat16),
                pltpu.VMEM((chunks, tokens, width), jnp.bfloat16),
                pltpu.VMEM((chunks, tokens, width), jnp.bfloat16),
                pltpu.VMEM((rows, columns), jnp.float32),
                pltpu.SemaphoreType.DMA((zs * chunks + 3 * chunks + 4 + chunks,)),
            ],
        ),
        out_shape=[out] * (zs * chunks),
        compiler_params=pltpu.CompilerParams(vmem_limit_bytes=58 * 1024 * 1024),
        cost_estimate=pl.CostEstimate(
            flops=16 * tokens * rows * columns + 48 * tokens * tokens * columns,
            bytes_accessed=16 * 1024 * 1024,
            transcendentals=16 * tokens * tokens * columns // HEAD,
        ),
    )(place, *inputs, *docs)
    return [found[:zs], found[zs:]]


def all_x(block):
    x = lax.axis_index("x")
    size = lax.axis_size("x")
    found = jnp.stack([block] + [shift(block, "x", by) for by in range(1, size)])
    return [lax.dynamic_index_in_dim(found, (x - i) % size, 0, False) for i in range(size)]


def sum_for_x(pieces):
    x = lax.axis_index("x")
    size = lax.axis_size("x")
    sent = [shift(pieces((x + by) % size), "x", by) for by in range(1, size)]
    total = pieces(x).astype(jnp.float32)
    for got in sent:
        total = total + got.astype(jnp.float32)
    return total


def ring_gather(block):
    size = lax.axis_size("z")
    found = [block] * size
    up = down = block
    for hop in range(1, size // 2 + 1):
        up = found[hop] = shift(up, "z", 1)
        if 2 * hop < size:
            down = found[size - hop] = shift(down, "z", -1)
    return found


def ring_sum(blocks):
    size = lax.axis_size("z")
    add = lambda a, b: a.astype(jnp.float32) + b.astype(jnp.float32)
    up, down = blocks[size // 2], blocks[size // 2 + 1]
    for hop in range(size // 2, 0, -1):
        up = shift(up, "z", 1)
        if hop > 1:
            up = add(up, blocks[hop - 1]).astype(jnp.bfloat16)
            down = shift(down, "z", -1)
            if hop > 2:
                down = add(down, blocks[size + 2 - hop]).astype(jnp.bfloat16)
    return add(up, down) + blocks[0].astype(jnp.float32)


def adam(weight, moment, second, grad):
    moment = BETA_ONE * moment + (1.0 - BETA_ONE) * grad
    second = BETA_TWO * second + (1.0 - BETA_TWO) * grad * grad
    weight = weight - LEARN_RATE * (moment / (jnp.sqrt(second) + EPSILON) + DECAY_RATE * weight)
    return weight, moment, second


def outer_merge(fragment, global_weight, outer_momentum, outer_delta):
    frag_cols = global_weight.shape[1] // FRAGS
    start = fragment[0] % FRAGS * frag_cols
    piece = lax.dynamic_slice_in_dim(outer_delta[0], start, frag_cols, 1)
    old_global = lax.dynamic_slice_in_dim(global_weight, start, frag_cols, 1)
    old_moment = lax.dynamic_slice_in_dim(outer_momentum, start, frag_cols, 1)
    count = 1
    for axis in REPLICA:
        piece = piece + shift(piece, axis, 1)
        count *= lax.axis_size(axis)
    mean = piece / count
    fresh_moment = OUTER_MU * old_moment + mean
    fresh_global = old_global - OUTER_RATE * (mean + OUTER_MU * fresh_moment)
    new_global = lax.dynamic_update_slice_in_dim(global_weight, fresh_global, start, 1)
    new_momentum = lax.dynamic_update_slice_in_dim(outer_momentum, fresh_moment, start, 1)
    return (start, fresh_global, new_global, new_momentum)


def on_device(
    features,
    queries,
    values,
    out_grad,
    doc_ids,
    fragment,
    local_weight,
    first_moment,
    second_moment,
    global_weight,
    outer_momentum,
    outer_delta,
):
    yh = lax.axis_index("yh")
    place = jnp.stack([yh, lax.axis_index("z")]).astype(jnp.int32)
    columns = local_weight.shape[2] // 2
    owned = local_weight.shape[1]

    def mine(array, wide=columns):
        return lax.dynamic_slice_in_dim(array, yh * wide, wide, array.ndim - 1)

    def theirs(array, wide=columns):
        return lax.dynamic_slice_in_dim(array, (1 - yh) * wide, wide, array.ndim - 1)

    def in_order(kept, got):
        first = jnp.where(yh == 0, kept, got)
        last = jnp.where(yh == 0, got, kept)
        return jnp.concatenate([first, last], axis=0)

    def paired(array):
        return in_order(mine(array), shift(theirs(array), "yh", 1))

    weight, moment, second = local_weight[0], first_moment[0], second_moment[0]

    def after(array, earlier):
        return lax.optimization_barrier((array, earlier))[0]

    def pack(arrays, c):
        widths = (WIDE * GROUP, WIDE * GROUP, WIDE)
        at = (1 - yh) * 2 + c
        parts = [lax.dynamic_slice_in_dim(a, at * w, w, 1) for a, w in zip(arrays, widths)]
        return jnp.concatenate(parts, axis=1)

    def send_features(step, earlier):
        return shift(after(features[0, step], earlier), "yh", 1)

    def send_pack(step, c, earlier):
        arrays = [a[0, step] for a in after((queries, out_grad, values), earlier)]
        return shift(pack(arrays, c), "yh", 1)

    def gather(rows):
        return ring_gather(rows[:, :WIDE]), ring_gather(rows[:, WIDE:])

    def terms(step, blocks, others, ready):
        own = (features, after(features[0, step], ready).T, queries, out_grad, values)
        f, *packs = others
        pair_docs = (doc_ids[0, step], docs[step])
        return weight_terms(step, blocks, own, (f, f.T, *packs), pair_docs, place)

    def scatter(blocks, earlier):
        part = jnp.concatenate([ring_sum(b).astype(jnp.bfloat16) for b in blocks], axis=1)
        part = after(part, earlier)
        part = part.reshape(lax.axis_size("x"), -1, part.shape[1])
        return sum_for_x(lambda i: lax.dynamic_index_in_dim(part, i, 0, False))

    def traded(grad):
        kept = jnp.where(yh == 0, grad[:owned], grad[owned:])
        got = shift(jnp.where(yh == 0, grad[owned:], grad[:owned]), "yh", 1)
        left = jnp.where(yh == 0, kept, got)
        right = jnp.where(yh == 0, got, kept)
        return jnp.concatenate([left, right], axis=1)

    sent = theirs(weight.astype(jnp.bfloat16))
    sent = jnp.concatenate([sent, doc_ids.reshape(1, columns).astype(jnp.bfloat16)], axis=0)
    got = shift(sent, "yh", 1)
    block = in_order(mine(weight.astype(jnp.bfloat16)), got[:owned])
    docs = got[owned].reshape(doc_ids.shape[1:]).astype(jnp.int32)
    rows = jnp.concatenate(all_x(block))
    first = [send_features(0, sent), send_pack(0, 0, rows), send_pack(0, 1, rows)]
    state = after(jnp.stack([weight, moment, second]), first)
    kept, got = mine(state), shift(theirs(state), "yh", 1)
    state = jnp.concatenate([jnp.where(yh == 0, kept, got), jnp.where(yh == 0, got, kept)], axis=1)
    early = send_pack(1, 0, rows)
    other_features = send_features(1, early)

    found = terms(0, gather(rows), first, rows)
    grad = scatter(after(found, early), other_features)
    fresh = adam(*state, grad)
    rows = jnp.concatenate(all_x(fresh[0].astype(jnp.bfloat16)))
    later = [other_features, early, send_pack(1, 1, rows)]
    outer = after((global_weight, outer_momentum, outer_delta), later)
    outcome = outer_merge(fragment, *outer)
    found = terms(1, gather(rows), later, found)
    own_grad = traded(after(grad, found))
    weight, moment, second = adam(weight, moment, second, own_grad)
    own_grad = traded(scatter(found, outcome))
    weight, moment, second = adam(weight, moment, second, own_grad)

    start, fresh_global, new_global, new_momentum = outcome
    frag_cols = fresh_global.shape[1]
    local_frag = lax.dynamic_slice_in_dim(weight, start, frag_cols, 1)
    merged = MERGE_RATE * local_frag + (1.0 - MERGE_RATE) * fresh_global
    weight = lax.dynamic_update_slice_in_dim(weight, merged, start, 1)
    return (weight[None], moment[None], second[None], new_global, new_momentum)


def solution(mesh):
    lattice = Mesh(mesh.devices.reshape(2, 2, 8, 4, 2), REPLICA + FSDP)
    tokens = P(REPLICA, None, FSDP, None)
    shards = P(REPLICA, FSDP, None)
    return jax.shard_map(
        on_device,
        mesh=lattice,
        in_specs=(
            tokens,
            tokens,
            tokens,
            tokens,
            P(REPLICA, None, FSDP),
            P(),
            shards,
            shards,
            shards,
            P(FSDP, None),
            P(FSDP, None),
            shards,
        ),
        out_specs=(shards, shards, shards, P(FSDP, None), P(FSDP, None)),
        check_vma=False,
    )
```

```python
import functools

import jax
import jax.numpy as jnp
from jax import lax
from jax.experimental import pallas as pl
from jax.experimental.pallas import tpu as pltpu
from jax.sharding import Mesh
from jax.sharding import PartitionSpec as P

HEAD = 128
STEPS = 2
FRAGS = 4
GROUP = 2
WIDE = 256

LEARN_RATE = 0.1
DECAY_RATE = 0.1
BETA_ONE = 0.9
BETA_TWO = 0.999
EPSILON = 1e-08
OUTER_MU = 0.9
OUTER_RATE = 0.7
MERGE_RATE = 0.5
SOFT_CAP = 50.0
QUERY_SCALE = 1.0 / 12.0

FSDP = ("z", "x", "yh")
REPLICA = ("yl", "core")


def shift(array, axis, by):
    size = lax.axis_size(axis)
    return lax.ppermute(array, axis, [(i, (i + by) % size) for i in range(size)])


def dot(a, b, dims):
    return lax.dot_general(a, b, (dims, ((), ())), preferred_element_type=jnp.float32)


def attend(key, query_heads, value, grad_heads, allowed):
    total = None
    for query, grad in zip(query_heads, grad_heads):
        capped = jnp.tanh(dot(key, query, ((1,), (1,))) * (QUERY_SCALE / SOFT_CAP))
        expo = jnp.where(allowed, jnp.exp(SOFT_CAP * capped), 0.0)
        probs = expo * (1.0 / jnp.sum(expo, axis=0, keepdims=True))
        dprob = dot(value, grad, ((1,), (1,)))
        inner = jnp.sum(probs * dprob, axis=0, keepdims=True)
        dscore = (probs * (dprob - inner) * (1.0 - capped * capped)).astype(jnp.bfloat16)
        term = dot(dscore, query, ((1,), (0,)))
        total = term if total is None else total + term
    return (total * QUERY_SCALE).astype(jnp.bfloat16)


def grad_kernel(factor, step, held, place, *refs):
    zs, chunks = 8, 2
    blocks, refs = refs[: zs * chunks], refs[zs * chunks :]
    (f, ft, q, g, v, other_f, other_ft), refs = refs[:7], refs[7:]
    packs, refs = refs[:held], refs[held:]
    docs, refs = refs[:4], refs[4:]
    outs, refs = refs[: zs * chunks], refs[zs * chunks :]
    weight, f_buf, ft_buf, own_buf, pack_buf, total_ref, sems = refs
    half, z = place[0], place[1]
    share = weight.shape[1] // zs
    wide = WIDE * GROUP
    spot = lambda i: pl.ds(pl.multiple_of(lax.rem(i + zs, zs) * share, share), share)
    copies = []

    def fetch(source, target):
        copies.append(pltpu.make_async_copy(source, target, sems.at[len(copies)]))
        copies[-1].start()
        return copies[-1]

    def fetch_weight(c):
        return [
            fetch(blocks[c * zs + by], weight.at[c, spot(z - by), :]) for by in range(zs)
        ]

    def fetch_own(c):
        start = 0
        found = []
        for source, width in ((q, wide), (g, wide), (v, WIDE)):
            at = pl.multiple_of((half * chunks + c) * width, width)
            found.append(
                fetch(
                    source.at[0, step, :, pl.ds(at, width)],
                    own_buf.at[c, :, start : start + width],
                )
            )
            start += width
        return found

    def fetch_pack(c):
        width = pack_buf.shape[2]
        source = packs[c] if held > 1 else packs[0].at[:, c * width : (c + 1) * width]
        return [fetch(source, pack_buf.at[c])]

    need = {}
    need["f", 0] = [fetch(f.at[0, step], f_buf.at[0])]
    need["w", 0] = fetch_weight(0)
    need["x", 0, 0] = fetch_own(0)
    need["ft", 0] = [fetch(ft, ft_buf.at[0])]
    need["f", 1] = [fetch(other_f, f_buf.at[1])]
    need["x", 0, 1] = fetch_pack(0)
    need["ft", 1] = [fetch(other_ft, ft_buf.at[1])]
    need["w", 1] = fetch_weight(1)
    need["x", 1, 0] = fetch_own(1)
    need["x", 1, 1] = fetch_pack(1)

    def wait(*key):
        for copy in need.pop(key, ()):
            copy.wait()

    for c in range(chunks):
        for n, buf in enumerate((own_buf, pack_buf)):
            wait("f", n)
            wait("w", c)
            keys = dot(f_buf[n], weight[c], ((1,), (0,)))
            keys = (keys * factor).astype(jnp.bfloat16)
            length = keys.shape[0]
            key_place = lax.broadcasted_iota(jnp.int32, (length, length), 0)
            query_place = lax.broadcasted_iota(jnp.int32, (length, length), 1)
            allowed = (key_place <= query_place) & (docs[n][...] == docs[2 + n][...])
            wait("x", c, n)
            at = lambda start, i: buf[c, :, start + i * HEAD : start + (i + 1) * HEAD]
            heads = []
            for h in range(WIDE // HEAD):
                members = range(h * GROUP, (h + 1) * GROUP)
                heads.append(
                    attend(
                        keys[:, h * HEAD : (h + 1) * HEAD],
                        [at(0, i) for i in members],
                        at(2 * wide, h),
                        [at(wide, i) for i in members],
                        allowed,
                    )
                )
            wait("ft", n)
            term = dot(ft_buf[n], jnp.concatenate(heads, axis=1), ((1,), (0,))) * factor
            total_ref[...] = term if n == 0 else total_ref[...] + term
        for by in range(zs):
            out = outs[c * zs + by]
            out[...] = total_ref[spot(z + by), :].astype(out.dtype)


def weight_terms(step, blocks, own, others, docs, place):
    zs, chunks = len(blocks[0]), len(blocks)
    share, columns = blocks[0][0].shape
    rows = share * zs
    tokens = others[0].shape[0]
    width = columns * (2 * GROUP + 1)
    whole = lambda *shape: pl.BlockSpec(shape, lambda i, p: (0,) * len(shape))
    inputs = [*blocks[0], *blocks[1], *own, *others]
    docs = [d.reshape(1, tokens) for d in docs] + [d.reshape(tokens, 1) for d in docs]
    out = jax.ShapeDtypeStruct((share, columns), jnp.bfloat16)
    found = pl.pallas_call(
        functools.partial(grad_kernel, rows ** (-0.5), step, len(others) - 2),
        grid_spec=pltpu.PrefetchScalarGridSpec(
            num_scalar_prefetch=1,
            grid=(1,),
            in_specs=[pl.BlockSpec(memory_space=pl.ANY)] * len(inputs)
            + [whole(*d.shape) for d in docs],
            out_specs=[whole(share, columns)] * (zs * chunks),
            scratch_shapes=[
                pltpu.VMEM((chunks, rows, columns), jnp.bfloat16),
                pltpu.VMEM((2, tokens, rows), jnp.bfloat16),
                pltpu.VMEM((2, rows, tokens), jnp.bfloat16),
                pltpu.VMEM((chunks, tokens, width), jnp.bfloat16),
                pltpu.VMEM((chunks, tokens, width), jnp.bfloat16),
                pltpu.VMEM((rows, columns), jnp.float32),
                pltpu.SemaphoreType.DMA((zs * chunks + 3 * chunks + 4 + chunks,)),
            ],
        ),
        out_shape=[out] * (zs * chunks),
        compiler_params=pltpu.CompilerParams(vmem_limit_bytes=58 * 1024 * 1024),
        cost_estimate=pl.CostEstimate(
            flops=16 * tokens * rows * columns + 48 * tokens * tokens * columns,
            bytes_accessed=16 * 1024 * 1024,
            transcendentals=16 * tokens * tokens * columns // HEAD,
        ),
    )(place, *inputs, *docs)
    return [found[:zs], found[zs:]]


def all_x(block):
    x = lax.axis_index("x")
    size = lax.axis_size("x")
    found = jnp.stack([block] + [shift(block, "x", by) for by in range(1, size)])
    return [lax.dynamic_index_in_dim(found, (x - i) % size, 0, False) for i in range(size)]


def sum_for_x(pieces):
    x = lax.axis_index("x")
    size = lax.axis_size("x")
    sent = [shift(pieces((x + by) % size), "x", by) for by in range(1, size)]
    total = pieces(x).astype(jnp.float32)
    for got in sent:
        total = total + got.astype(jnp.float32)
    return total


def ring_gather(block):
    size = lax.axis_size("z")
    found = [block] * size
    up = down = block
    for hop in range(1, size // 2 + 1):
        up = found[hop] = shift(up, "z", 1)
        if 2 * hop < size:
            down = found[size - hop] = shift(down, "z", -1)
    return found


def ring_sum(blocks):
    size = lax.axis_size("z")
    add = lambda a, b: a.astype(jnp.float32) + b.astype(jnp.float32)
    up, down = blocks[size // 2], blocks[size // 2 + 1]
    for hop in range(size // 2, 0, -1):
        up = shift(up, "z", 1)
        if hop > 1:
            up = add(up, blocks[hop - 1]).astype(jnp.bfloat16)
            down = shift(down, "z", -1)
            if hop > 2:
                down = add(down, blocks[size + 2 - hop]).astype(jnp.bfloat16)
    return add(up, down) + blocks[0].astype(jnp.float32)


def adam(weight, moment, second, grad):
    moment = BETA_ONE * moment + (1.0 - BETA_ONE) * grad
    second = BETA_TWO * second + (1.0 - BETA_TWO) * grad * grad
    weight = weight - LEARN_RATE * (moment / (jnp.sqrt(second) + EPSILON) + DECAY_RATE * weight)
    return weight, moment, second


def outer_merge(fragment, global_weight, outer_momentum, outer_delta):
    frag_cols = global_weight.shape[1] // FRAGS
    start = fragment[0] % FRAGS * frag_cols
    piece = lax.dynamic_slice_in_dim(outer_delta[0], start, frag_cols, 1)
    old_global = lax.dynamic_slice_in_dim(global_weight, start, frag_cols, 1)
    old_moment = lax.dynamic_slice_in_dim(outer_momentum, start, frag_cols, 1)
    count = 1
    for axis in REPLICA:
        piece = piece + shift(piece, axis, 1)
        count *= lax.axis_size(axis)
    mean = piece / count
    fresh_moment = OUTER_MU * old_moment + mean
    fresh_global = old_global - OUTER_RATE * (mean + OUTER_MU * fresh_moment)
    new_global = lax.dynamic_update_slice_in_dim(global_weight, fresh_global, start, 1)
    new_momentum = lax.dynamic_update_slice_in_dim(outer_momentum, fresh_moment, start, 1)
    return (start, fresh_global, new_global, new_momentum)


def on_device(
    features,
    queries,
    values,
    out_grad,
    doc_ids,
    fragment,
    local_weight,
    first_moment,
    second_moment,
    global_weight,
    outer_momentum,
    outer_delta,
):
    yh = lax.axis_index("yh")
    place = jnp.stack([yh, lax.axis_index("z")]).astype(jnp.int32)
    columns = local_weight.shape[2] // 2
    owned = local_weight.shape[1]

    def mine(array, wide=columns):
        return lax.dynamic_slice_in_dim(array, yh * wide, wide, array.ndim - 1)

    def theirs(array, wide=columns):
        return lax.dynamic_slice_in_dim(array, (1 - yh) * wide, wide, array.ndim - 1)

    def in_order(kept, got):
        first = jnp.where(yh == 0, kept, got)
        last = jnp.where(yh == 0, got, kept)
        return jnp.concatenate([first, last], axis=0)

    def paired(array):
        return in_order(mine(array), shift(theirs(array), "yh", 1))

    weight, moment, second = local_weight[0], first_moment[0], second_moment[0]

    def after(array, earlier):
        return lax.optimization_barrier((array, earlier))[0]

    def pack(arrays, c):
        widths = (WIDE * GROUP, WIDE * GROUP, WIDE)
        at = (1 - yh) * 2 + c
        parts = [lax.dynamic_slice_in_dim(a, at * w, w, 1) for a, w in zip(arrays, widths)]
        return jnp.concatenate(parts, axis=1)

    def send_features(step, earlier):
        return shift(after(features[0, step], earlier), "yh", 1)

    def send_pack(step, chosen, earlier):
        arrays = [a[0, step] for a in after((queries, out_grad, values), earlier)]
        return shift(jnp.concatenate([pack(arrays, c) for c in chosen], axis=1), "yh", 1)

    def gather(rows):
        return ring_gather(rows[:, :WIDE]), ring_gather(rows[:, WIDE:])

    def terms(step, blocks, others, ready):
        own = (features, after(features[0, step], ready).T, queries, out_grad, values)
        f, *packs = others
        pair_docs = (doc_ids[0, step], docs[step])
        return weight_terms(step, blocks, own, (f, f.T, *packs), pair_docs, place)

    def scatter(blocks, earlier):
        part = jnp.concatenate([ring_sum(b).astype(jnp.bfloat16) for b in blocks], axis=1)
        part = after(part, earlier)
        part = part.reshape(lax.axis_size("x"), -1, part.shape[1])
        return sum_for_x(lambda i: lax.dynamic_index_in_dim(part, i, 0, False))

    def traded(grad):
        kept = jnp.where(yh == 0, grad[:owned], grad[owned:])
        got = shift(jnp.where(yh == 0, grad[owned:], grad[:owned]), "yh", 1)
        left = jnp.where(yh == 0, kept, got)
        right = jnp.where(yh == 0, got, kept)
        return jnp.concatenate([left, right], axis=1)

    sent = theirs(weight.astype(jnp.bfloat16))
    sent = jnp.concatenate([sent, doc_ids.reshape(1, columns).astype(jnp.bfloat16)], axis=0)
    got = shift(sent, "yh", 1)
    block = in_order(mine(weight.astype(jnp.bfloat16)), got[:owned])
    docs = got[owned].reshape(doc_ids.shape[1:]).astype(jnp.int32)
    rows = jnp.concatenate(all_x(block))
    first = [send_features(0, sent), send_pack(0, (0, 1), rows)]
    state = after(jnp.stack([weight, moment, second]), first)
    kept, got = mine(state), shift(theirs(state), "yh", 1)
    state = jnp.concatenate([jnp.where(yh == 0, kept, got), jnp.where(yh == 0, got, kept)], axis=1)
    early = send_pack(1, (0,), rows)
    other_features = send_features(1, early)

    found = terms(0, gather(rows), first, rows)
    grad = scatter(after(found, early), other_features)
    fresh = adam(*state, grad)
    rows = jnp.concatenate(all_x(fresh[0].astype(jnp.bfloat16)))
    later = [other_features, early, send_pack(1, (1,), early)]
    outer = after((global_weight, outer_momentum, outer_delta), later)
    outcome = outer_merge(fragment, *outer)
    found = terms(1, gather(rows), later, found)
    own_grad = traded(after(grad, found))
    weight, moment, second = adam(weight, moment, second, own_grad)
    own_grad = traded(scatter(found, outcome))
    weight, moment, second = adam(weight, moment, second, own_grad)

    start, fresh_global, new_global, new_momentum = outcome
    frag_cols = fresh_global.shape[1]
    local_frag = lax.dynamic_slice_in_dim(weight, start, frag_cols, 1)
    merged = MERGE_RATE * local_frag + (1.0 - MERGE_RATE) * fresh_global
    weight = lax.dynamic_update_slice_in_dim(weight, merged, start, 1)
    return (weight[None], moment[None], second[None], new_global, new_momentum)


def solution(mesh):
    lattice = Mesh(mesh.devices.reshape(2, 2, 8, 4, 2), REPLICA + FSDP)
    tokens = P(REPLICA, None, FSDP, None)
    shards = P(REPLICA, FSDP, None)
    return jax.shard_map(
        on_device,
        mesh=lattice,
        in_specs=(
            tokens,
            tokens,
            tokens,
            tokens,
            P(REPLICA, None, FSDP),
            P(),
            shards,
            shards,
            shards,
            P(FSDP, None),
            P(FSDP, None),
            shards,
        ),
        out_specs=(shards, shards, shards, P(FSDP, None), P(FSDP, None)),
        check_vma=False,
    )
```

```python
import functools

import jax
import jax.numpy as jnp
from jax import lax
from jax.experimental import pallas as pl
from jax.experimental.pallas import tpu as pltpu
from jax.sharding import Mesh
from jax.sharding import PartitionSpec as P

HEAD = 128
STEPS = 2
FRAGS = 4
GROUP = 2
WIDE = 256

LEARN_RATE = 0.1
DECAY_RATE = 0.1
BETA_ONE = 0.9
BETA_TWO = 0.999
EPSILON = 1e-08
OUTER_MU = 0.9
OUTER_RATE = 0.7
MERGE_RATE = 0.5
SOFT_CAP = 50.0
QUERY_SCALE = 1.0 / 12.0

FSDP = ("z", "x", "yh")
REPLICA = ("yl", "core")


def shift(array, axis, by):
    size = lax.axis_size(axis)
    return lax.ppermute(array, axis, [(i, (i + by) % size) for i in range(size)])


def dot(a, b, dims):
    return lax.dot_general(a, b, (dims, ((), ())), preferred_element_type=jnp.float32)


def attend(key, query_heads, value, grad_heads, allowed):
    total = None
    for query, grad in zip(query_heads, grad_heads):
        capped = jnp.tanh(dot(key, query, ((1,), (1,))) * (QUERY_SCALE / SOFT_CAP))
        expo = jnp.where(allowed, jnp.exp(SOFT_CAP * capped), 0.0)
        probs = expo * (1.0 / jnp.sum(expo, axis=0, keepdims=True))
        dprob = dot(value, grad, ((1,), (1,)))
        inner = jnp.sum(probs * dprob, axis=0, keepdims=True)
        dscore = (probs * (dprob - inner) * (1.0 - capped * capped)).astype(jnp.bfloat16)
        term = dot(dscore, query, ((1,), (0,)))
        total = term if total is None else total + term
    return (total * QUERY_SCALE).astype(jnp.bfloat16)


def grad_kernel(factor, step, held, place, *refs):
    zs, chunks = 8, 2
    blocks, refs = refs[: zs * chunks], refs[zs * chunks :]
    (f, ft, q, g, v, other_f, other_ft), refs = refs[:7], refs[7:]
    packs, refs = refs[:held], refs[held:]
    docs, refs = refs[:4], refs[4:]
    outs, refs = refs[: zs * chunks], refs[zs * chunks :]
    weight, f_buf, ft_buf, own_buf, pack_buf, total_ref, sems = refs
    half, z = place[0], place[1]
    share = weight.shape[1] // zs
    wide = WIDE * GROUP
    spot = lambda i: pl.ds(pl.multiple_of(lax.rem(i + zs, zs) * share, share), share)
    copies = []

    def fetch(source, target):
        copies.append(pltpu.make_async_copy(source, target, sems.at[len(copies)]))
        copies[-1].start()
        return copies[-1]

    def fetch_weight(c):
        return [
            fetch(blocks[c * zs + by], weight.at[c, spot(z - by), :]) for by in range(zs)
        ]

    def fetch_own(c):
        start = 0
        found = []
        for source, width in ((q, wide), (g, wide), (v, WIDE)):
            at = pl.multiple_of((half * chunks + c) * width, width)
            found.append(
                fetch(
                    source.at[0, step, :, pl.ds(at, width)],
                    own_buf.at[c, :, start : start + width],
                )
            )
            start += width
        return found

    def fetch_pack(c):
        width = pack_buf.shape[2]
        source = packs[c] if held > 1 else packs[0].at[:, c * width : (c + 1) * width]
        return [fetch(source, pack_buf.at[c])]

    need = {}
    need["f", 0] = [fetch(f.at[0, step], f_buf.at[0])]
    need["w", 0] = fetch_weight(0)
    need["x", 0, 0] = fetch_own(0)
    need["ft", 0] = [fetch(ft, ft_buf.at[0])]
    need["f", 1] = [fetch(other_f, f_buf.at[1])]
    need["x", 0, 1] = fetch_pack(0)
    need["ft", 1] = [fetch(other_ft, ft_buf.at[1])]
    need["w", 1] = fetch_weight(1)
    need["x", 1, 0] = fetch_own(1)
    need["x", 1, 1] = fetch_pack(1)

    def wait(*key):
        for copy in need.pop(key, ()):
            copy.wait()

    for c in range(chunks):
        for n, buf in enumerate((own_buf, pack_buf)):
            wait("f", n)
            wait("w", c)
            keys = dot(f_buf[n], weight[c], ((1,), (0,)))
            keys = (keys * factor).astype(jnp.bfloat16)
            length = keys.shape[0]
            key_place = lax.broadcasted_iota(jnp.int32, (length, length), 0)
            query_place = lax.broadcasted_iota(jnp.int32, (length, length), 1)
            allowed = (key_place <= query_place) & (docs[n][...] == docs[2 + n][...])
            wait("x", c, n)
            at = lambda start, i: buf[c, :, start + i * HEAD : start + (i + 1) * HEAD]
            heads = []
            for h in range(WIDE // HEAD):
                members = range(h * GROUP, (h + 1) * GROUP)
                heads.append(
                    attend(
                        keys[:, h * HEAD : (h + 1) * HEAD],
                        [at(0, i) for i in members],
                        at(2 * wide, h),
                        [at(wide, i) for i in members],
                        allowed,
                    )
                )
            wait("ft", n)
            term = dot(ft_buf[n], jnp.concatenate(heads, axis=1), ((1,), (0,))) * factor
            total_ref[...] = term if n == 0 else total_ref[...] + term
        for by in range(zs):
            out = outs[c * zs + by]
            out[...] = total_ref[spot(z + by), :].astype(out.dtype)


def weight_terms(step, blocks, own, others, docs, place):
    zs, chunks = len(blocks[0]), len(blocks)
    share, columns = blocks[0][0].shape
    rows = share * zs
    tokens = others[0].shape[0]
    width = columns * (2 * GROUP + 1)
    whole = lambda *shape: pl.BlockSpec(shape, lambda i, p: (0,) * len(shape))
    inputs = [*blocks[0], *blocks[1], *own, *others]
    docs = [d.reshape(1, tokens) for d in docs] + [d.reshape(tokens, 1) for d in docs]
    out = jax.ShapeDtypeStruct((share, columns), jnp.bfloat16)
    found = pl.pallas_call(
        functools.partial(grad_kernel, rows ** (-0.5), step, len(others) - 2),
        grid_spec=pltpu.PrefetchScalarGridSpec(
            num_scalar_prefetch=1,
            grid=(1,),
            in_specs=[pl.BlockSpec(memory_space=pl.ANY)] * len(inputs)
            + [whole(*d.shape) for d in docs],
            out_specs=[whole(share, columns)] * (zs * chunks),
            scratch_shapes=[
                pltpu.VMEM((chunks, rows, columns), jnp.bfloat16),
                pltpu.VMEM((2, tokens, rows), jnp.bfloat16),
                pltpu.VMEM((2, rows, tokens), jnp.bfloat16),
                pltpu.VMEM((chunks, tokens, width), jnp.bfloat16),
                pltpu.VMEM((chunks, tokens, width), jnp.bfloat16),
                pltpu.VMEM((rows, columns), jnp.float32),
                pltpu.SemaphoreType.DMA((zs * chunks + 3 * chunks + 4 + chunks,)),
            ],
        ),
        out_shape=[out] * (zs * chunks),
        compiler_params=pltpu.CompilerParams(vmem_limit_bytes=58 * 1024 * 1024),
        cost_estimate=pl.CostEstimate(
            flops=16 * tokens * rows * columns + 48 * tokens * tokens * columns,
            bytes_accessed=16 * 1024 * 1024,
            transcendentals=16 * tokens * tokens * columns // HEAD,
        ),
    )(place, *inputs, *docs)
    return [found[:zs], found[zs:]]


def all_x(block):
    x = lax.axis_index("x")
    size = lax.axis_size("x")
    found = jnp.stack([block] + [shift(block, "x", by) for by in range(1, size)])
    return [lax.dynamic_index_in_dim(found, (x - i) % size, 0, False) for i in range(size)]


def sum_for_x(pieces):
    x = lax.axis_index("x")
    size = lax.axis_size("x")
    sent = [shift(pieces((x + by) % size), "x", by) for by in range(1, size)]
    total = pieces(x).astype(jnp.float32)
    for got in sent:
        total = total + got.astype(jnp.float32)
    return total


def ring_gather(block):
    size = lax.axis_size("z")
    found = [block] * size
    up = down = block
    for hop in range(1, size // 2 + 1):
        up = found[hop] = shift(up, "z", 1)
        if 2 * hop < size:
            down = found[size - hop] = shift(down, "z", -1)
    return found


def ring_sum(blocks):
    size = lax.axis_size("z")
    add = lambda a, b: a.astype(jnp.float32) + b.astype(jnp.float32)
    up, down = blocks[size // 2], blocks[size // 2 + 1]
    for hop in range(size // 2, 0, -1):
        up = shift(up, "z", 1)
        if hop > 1:
            up = add(up, blocks[hop - 1]).astype(jnp.bfloat16)
            down = shift(down, "z", -1)
            if hop > 2:
                down = add(down, blocks[size + 2 - hop]).astype(jnp.bfloat16)
    return add(up, down) + blocks[0].astype(jnp.float32)


def adam(weight, moment, second, grad):
    moment = BETA_ONE * moment + (1.0 - BETA_ONE) * grad
    second = BETA_TWO * second + (1.0 - BETA_TWO) * grad * grad
    weight = weight - LEARN_RATE * (moment / (jnp.sqrt(second) + EPSILON) + DECAY_RATE * weight)
    return weight, moment, second


def outer_merge(fragment, global_weight, outer_momentum, outer_delta):
    frag_cols = global_weight.shape[1] // FRAGS
    start = fragment[0] % FRAGS * frag_cols
    piece = lax.dynamic_slice_in_dim(outer_delta[0], start, frag_cols, 1)
    old_global = lax.dynamic_slice_in_dim(global_weight, start, frag_cols, 1)
    old_moment = lax.dynamic_slice_in_dim(outer_momentum, start, frag_cols, 1)
    count = 1
    for axis in REPLICA:
        piece = piece + shift(piece, axis, 1)
        count *= lax.axis_size(axis)
    mean = piece / count
    fresh_moment = OUTER_MU * old_moment + mean
    fresh_global = old_global - OUTER_RATE * (mean + OUTER_MU * fresh_moment)
    new_global = lax.dynamic_update_slice_in_dim(global_weight, fresh_global, start, 1)
    new_momentum = lax.dynamic_update_slice_in_dim(outer_momentum, fresh_moment, start, 1)
    return (start, fresh_global, new_global, new_momentum)


def on_device(
    features,
    queries,
    values,
    out_grad,
    doc_ids,
    fragment,
    local_weight,
    first_moment,
    second_moment,
    global_weight,
    outer_momentum,
    outer_delta,
):
    yh = lax.axis_index("yh")
    place = jnp.stack([yh, lax.axis_index("z")]).astype(jnp.int32)
    columns = local_weight.shape[2] // 2
    owned = local_weight.shape[1]

    def mine(array, wide=columns):
        return lax.dynamic_slice_in_dim(array, yh * wide, wide, array.ndim - 1)

    def theirs(array, wide=columns):
        return lax.dynamic_slice_in_dim(array, (1 - yh) * wide, wide, array.ndim - 1)

    def in_order(kept, got):
        first = jnp.where(yh == 0, kept, got)
        last = jnp.where(yh == 0, got, kept)
        return jnp.concatenate([first, last], axis=0)

    def paired(array):
        return in_order(mine(array), shift(theirs(array), "yh", 1))

    weight, moment, second = local_weight[0], first_moment[0], second_moment[0]

    def after(array, earlier):
        return lax.optimization_barrier((array, earlier))[0]

    def pack(arrays, c):
        widths = (WIDE * GROUP, WIDE * GROUP, WIDE)
        at = (1 - yh) * 2 + c
        parts = [lax.dynamic_slice_in_dim(a, at * w, w, 1) for a, w in zip(arrays, widths)]
        return jnp.concatenate(parts, axis=1)

    def send_features(step, earlier):
        return shift(after(features[0, step], earlier), "yh", 1)

    def send_pack(step, chosen, earlier):
        arrays = [a[0, step] for a in after((queries, out_grad, values), earlier)]
        return shift(jnp.concatenate([pack(arrays, c) for c in chosen], axis=1), "yh", 1)

    def gather(rows):
        return ring_gather(rows[:, :WIDE]), ring_gather(rows[:, WIDE:])

    def terms(step, blocks, others, ready):
        own = (features, after(features[0, step], ready).T, queries, out_grad, values)
        f, *packs = others
        pair_docs = (doc_ids[0, step], docs[step])
        return weight_terms(step, blocks, own, (f, f.T, *packs), pair_docs, place)

    def scatter(blocks, earlier):
        part = jnp.concatenate([ring_sum(b).astype(jnp.bfloat16) for b in blocks], axis=1)
        part = after(part, earlier)
        part = part.reshape(lax.axis_size("x"), -1, part.shape[1])
        return sum_for_x(lambda i: lax.dynamic_index_in_dim(part, i, 0, False))

    def traded(grad):
        kept = jnp.where(yh == 0, grad[:owned], grad[owned:])
        got = shift(jnp.where(yh == 0, grad[owned:], grad[:owned]), "yh", 1)
        left = jnp.where(yh == 0, kept, got)
        right = jnp.where(yh == 0, got, kept)
        return jnp.concatenate([left, right], axis=1)

    sent = theirs(weight.astype(jnp.bfloat16))
    sent = jnp.concatenate([sent, doc_ids.reshape(1, columns).astype(jnp.bfloat16)], axis=0)
    got = shift(sent, "yh", 1)
    block = in_order(mine(weight.astype(jnp.bfloat16)), got[:owned])
    docs = got[owned].reshape(doc_ids.shape[1:]).astype(jnp.int32)
    rows = jnp.concatenate(all_x(block))
    first = [send_features(0, sent), send_pack(0, (0, 1), rows)]
    state = after(jnp.stack([weight, moment, second]), first)
    kept, got = mine(state), shift(theirs(state), "yh", 1)
    state = jnp.concatenate([jnp.where(yh == 0, kept, got), jnp.where(yh == 0, got, kept)], axis=1)
    early = send_pack(1, (0,), rows)
    other_features = send_features(1, early)

    found = terms(0, gather(rows), first, rows)
    found = after(found, early)
    late = send_pack(1, (1,), found)
    grad = scatter(found, other_features)
    fresh = adam(*state, grad)
    rows = jnp.concatenate(all_x(fresh[0].astype(jnp.bfloat16)))
    later = [other_features, early, late]
    outer = after((global_weight, outer_momentum, outer_delta), later)
    outcome = outer_merge(fragment, *outer)
    found = terms(1, gather(rows), later, found)
    own_grad = traded(after(grad, found))
    weight, moment, second = adam(weight, moment, second, own_grad)
    own_grad = traded(scatter(found, outcome))
    weight, moment, second = adam(weight, moment, second, own_grad)

    start, fresh_global, new_global, new_momentum = outcome
    frag_cols = fresh_global.shape[1]
    local_frag = lax.dynamic_slice_in_dim(weight, start, frag_cols, 1)
    merged = MERGE_RATE * local_frag + (1.0 - MERGE_RATE) * fresh_global
    weight = lax.dynamic_update_slice_in_dim(weight, merged, start, 1)
    return (weight[None], moment[None], second[None], new_global, new_momentum)


def solution(mesh):
    lattice = Mesh(mesh.devices.reshape(2, 2, 8, 4, 2), REPLICA + FSDP)
    tokens = P(REPLICA, None, FSDP, None)
    shards = P(REPLICA, FSDP, None)
    return jax.shard_map(
        on_device,
        mesh=lattice,
        in_specs=(
            tokens,
            tokens,
            tokens,
            tokens,
            P(REPLICA, None, FSDP),
            P(),
            shards,
            shards,
            shards,
            P(FSDP, None),
            P(FSDP, None),
            shards,
        ),
        out_specs=(shards, shards, shards, P(FSDP, None), P(FSDP, None)),
        check_vma=False,
    )
```
